128 devices in a mesh: depth: 32 (over y, x, core), tile: 4 (over z).
Axes of the slice: x: 4, y: 4, z: 4, core: 2. Of those that a mesh axis runs over, the one named last changes fastest.
Arguments:
- scalar_field: float32 [512, 4, 512, 512], P('depth', 'tile'), may hold values from -12 to 12
- depth_rank: int32 [32, 4], P('depth', 'tile'), may hold values from 0 to 31, as said below
- palette: float32 [3, 2], replicated, may hold values from -1.5 to 1.5
- extinction: float32 [2], replicated, may hold values from 0.4 to 1.6
Outputs:
- scanline_image: float32 [4, 1, 512, 2048], P(None, None, ('depth', 'tile'))
The draws below stay inside these ranges and needn't reach their ends.
Inputs may be any that keep to these rules, and one draw needn't show every extreme that they name: In every column of depth_rank each of 0 to 31 appears once, and for every k the depth indices that agree in their k lowest bits hold a contiguous range of ranks.
All inputs are finite; a program needn't handle non-finite values.
Results may differ from the reference program's by a relative error of at most 0.000034.
Values sent between devices are 32-bit elements; how exact they have to be, the bound alone decides.
No kernel may reach another device: no remote copies, remote signals or barrier semaphores. Data moves between devices by JAX's collectives and lax.ppermute only.
A program may use at most 256 MiB of HBM per device.

```python
import math
import jax
import jax.numpy as jnp
from jax import lax

BZ = 16
TY = 512
TX = 512
TILES_X = 4
TILES = 4
TILES_Y = 1
NZ = 512
N_DEPTH = 32
N_TILE = 4


def draw_depth_rank(key, part):
    key = jax.random.fold_in(key, 11)
    tree_depth = N_DEPTH.bit_length() - 1
    depth_index = jnp.arange(N_DEPTH, dtype=jnp.int32)
    rank_table = jnp.zeros((N_DEPTH, N_TILE), jnp.int32)
    for tree_level in range(tree_depth):
        flip_table = jax.random.randint(jax.random.fold_in(key, tree_level), (N_DEPTH, N_TILE), 0, 2).astype(jnp.int32)
        low_bits = depth_index & (1 << tree_level) - 1
        own_bit = depth_index >> tree_level & 1
        flipped = own_bit[:, None] ^ flip_table[low_bits, :]
        rank_table = rank_table + flipped * (1 << tree_depth - 1 - tree_level)
    return rank_table


def draw_scalar_field(key, part):
    key = jax.random.fold_in(key, 5)
    field_shape = (NZ, TILES, TY, TX)
    return jnp.clip(jax.random.normal(key, field_shape, jnp.float32), -6.0, 6.0)


def setup_inputs(seed: int = 0) -> dict:
    seeds = jax.random.split(jax.random.key(seed), 5)
    scalar_field = draw_scalar_field(jax.random.fold_in(seeds[4], 71), 0)
    depth_rank = draw_depth_rank(jax.random.fold_in(seeds[4], 71), 0)
    palette = jnp.clip(jax.random.uniform(seeds[2], (3, 2), jnp.float32, -1.5, 1.5), -1.5, 1.5)
    extinction = jnp.clip(jnp.exp(jax.random.uniform(seeds[3], (2,), jnp.float32, math.log(0.4), math.log(1.6))), 0.4, 1.6)
    return dict(scalar_field=scalar_field, depth_rank=depth_rank, palette=palette, extinction=extinction)


def composite_over(nearer, farther):
    return nearer + (1.0 - nearer[3:4]) * farther


def march_brick(samples_in, palette, extinction):
    slope = palette[:, 0][:, None, None, None]
    offset = palette[:, 1][:, None, None, None]

    def march_step(accumulated, sample_slice):
        rate = extinction[0] * sample_slice * sample_slice + extinction[1]
        opacity = 1.0 - jnp.exp(-rate / NZ)
        colour = jax.nn.sigmoid(slope * sample_slice[None] + offset)
        sample = jnp.concatenate([opacity[None] * colour, opacity[None]], axis=0)
        return composite_over(accumulated, sample), None

    start = jnp.zeros((4,) + samples_in.shape[1:], jnp.float32)
    result, _ = lax.scan(march_step, start, samples_in)
    return result


def reference(scalar_field, depth_rank, palette, extinction):
    partials = []
    for brick in range(N_DEPTH):
        partials.append(march_brick(scalar_field[brick * BZ:(brick + 1) * BZ], palette, extinction))
    composite = jnp.zeros_like(partials[0])
    for position in range(N_DEPTH):
        selector = (depth_rank == position).astype(jnp.float32)
        ordered_part = jnp.zeros_like(partials[0])
        for brick in range(N_DEPTH):
            ordered_part = ordered_part + selector[brick][None, :, None, None] * partials[brick]
        composite = composite_over(composite, ordered_part)
    arranged = composite.reshape(4, TILES_Y, TILES_X, TY, TX).transpose(0, 1, 3, 2, 4)
    return arranged.reshape(4, TILES_Y, TY, TILES_X * TX)
```

```python
import functools
import math

import jax
import jax.numpy as jnp
from jax import lax
from jax.experimental import pallas as pl
from jax.experimental.pallas import tpu as pltpu
from jax.sharding import PartitionSpec as P

N = 4
SAMPLES = 16
LANES = 128
BLOCKS = 4
CHANNELS = 4
SLAB = BLOCKS * 8
VMEM = 40 * 2**20


def merge_two(a, b, a_in_front):
    one = jnp.float32(1.0)
    weight_a = jnp.where(a_in_front, one, b[3])
    weight_b = jnp.where(a_in_front, a[3], one)
    return [a[k] * weight_a + b[k] * weight_b for k in range(3)] + [a[3] * b[3]]


def merge_four(parts, ranks):
    even = merge_two(parts[0], parts[2], (ranks[0] < ranks[2])[None])
    odd = merge_two(parts[1], parts[3], (ranks[1] < ranks[3])[None])
    return merge_two(even, odd, (ranks[0] < ranks[1])[None])


def read_slab(ref, start):
    return ref[pl.ds(pl.multiple_of(start, SLAB), SLAB), :].reshape(BLOCKS, 8, LANES)


def write_slab(ref, start, value):
    ref[pl.ds(start, SLAB), :] = value.reshape(SLAB, LANES)


def march_kernel(place, palette, extinction, rank, *refs, count, depth_total):
    fields, messages = refs[:count], refs[count:]
    x_block = pl.program_id(0)
    odd_z = (place[3] & 1) == 1
    scale = -1.0 / (depth_total * math.log(2.0))
    quadratic = extinction[0] * scale
    constant = extinction[1] * scale
    slopes = [palette[k, 0] * 0.5 for k in range(3)]
    offsets = [palette[k, 1] * 0.5 for k in range(3)]
    width = 2 * LANES
    low_half = lax.broadcasted_iota(jnp.int32, (8, width), 0) < 4

    for j in range(count):
        field, first, second = fields[j], messages[2 * j], messages[2 * j + 1]

        def columns(block, carry, field=field, first=first, second=second):
            lanes = pl.ds(pl.multiple_of(block * width, width), width)
            shape = (2, 8, width)
            squares = jnp.zeros(shape, jnp.float32)
            through = jnp.ones(shape, jnp.float32)
            totals = [jnp.zeros(shape, jnp.float32) for _ in range(3)]
            for i in range(SAMPLES):
                s = field[i, :, :, lanes]
                squares = squares + s * s
                after = jnp.exp2(squares * quadratic + constant * float(i + 1))
                weight = through - after
                through = after
                for k in range(3):
                    totals[k] = totals[k] + weight * jnp.tanh(s * slopes[k] + offsets[k])
            opacity = 1.0 - through
            channels = [0.5 * (opacity + totals[k]) for k in range(3)] + [through]
            for k in range(CHANNELS):
                near, far = channels[k][0], channels[k][1]
                low = jnp.where(low_half, near, pltpu.roll(far, 4, 0))
                high = jnp.where(low_half, pltpu.roll(near, 4, 0), far)
                for half in range(2):
                    part = slice(half * LANES, (half + 1) * LANES)
                    row = pl.multiple_of(((k * N + x_block) * BLOCKS + block * 2 + half) * 8, 8)
                    first[pl.ds(row, 8), :] = jnp.where(odd_z, high[:, part], low[:, part])
                    second[pl.ds(row, 8), :] = jnp.where(odd_z, low[:, part], high[:, part])
            return carry

        lax.fori_loop(0, BLOCKS // 2, columns, 0)

    @pl.when(x_block == 0)
    def _():
        own = jnp.full((8, LANES), rank[0, 0].astype(jnp.float32))
        for message in messages:
            message[pl.ds(CHANNELS * N * SLAB, 8), :] = own


def march(field, place, palette, extinction, rank, y_flips, z_pair, depth_total):
    count = len(y_flips)
    rows = CHANNELS * N * SLAB + 8

    def field_index(flip):
        return lambda x, where: (0, 0, where[0] ^ flip, x, 0, (where[3] >> 1) ^ z_pair, 0, 0)

    smem = pl.BlockSpec(memory_space=pltpu.SMEM)
    pixels = count * N * 2 * 8 * 512
    return pl.pallas_call(
        functools.partial(march_kernel, count=count, depth_total=depth_total),
        grid_spec=pltpu.PrefetchScalarGridSpec(
            num_scalar_prefetch=1,
            grid=(N,),
            in_specs=[smem, smem, smem]
            + [
                pl.BlockSpec((SAMPLES, None, None, None, 2, None, 8, 512), field_index(flip))
                for flip in y_flips
            ],
            out_specs=[pl.BlockSpec((rows, LANES), lambda x, where: (0, 0))] * (2 * count),
        ),
        out_shape=[jax.ShapeDtypeStruct((rows, LANES), jnp.float32)] * (2 * count),
        compiler_params=pltpu.CompilerParams(vmem_limit_bytes=VMEM),
        cost_estimate=pl.CostEstimate(
            flops=pixels * SAMPLES * 20,
            bytes_accessed=pixels * 4 * (SAMPLES + 4),
            transcendentals=pixels * SAMPLES * 4,
        ),
        name="march",
    )(place, palette, extinction, rank, *([field] * count))


def merge_y_kernel(place, *refs):
    inputs, outputs = refs[:8], refs[8:]
    for tile in range(2):
        group = inputs[tile * 4 : tile * 4 + 4]
        ranks = [m[pl.ds(CHANNELS * N * SLAB, 8), :] for m in group]
        for flip in range(N):
            x = place[1] ^ flip
            parts = [[read_slab(m, (k * N + x) * SLAB) for k in range(CHANNELS)] for m in group]
            merged = merge_four(parts, ranks)
            for k in range(CHANNELS):
                write_slab(outputs[flip], (tile * CHANNELS + k) * SLAB, merged[k])
            outputs[flip][pl.ds(2 * CHANNELS * SLAB + tile * 8, 8), :] = ranks[0]


def merge_y(place, messages):
    rows = 2 * CHANNELS * SLAB + 16
    vmem = pl.BlockSpec(memory_space=pltpu.VMEM)
    return pl.pallas_call(
        merge_y_kernel,
        in_specs=[pl.BlockSpec(memory_space=pltpu.SMEM)] + [vmem] * 8,
        out_specs=[vmem] * N,
        out_shape=[jax.ShapeDtypeStruct((rows, LANES), jnp.float32)] * N,
        compiler_params=pltpu.CompilerParams(vmem_limit_bytes=VMEM),
        cost_estimate=pl.CostEstimate(flops=2**21, bytes_accessed=3 * 2**20, transcendentals=0),
        name="merge_y",
    )(place, *messages)


def merge_x_kernel(*refs):
    inputs, out = refs[:-1], refs[-1]
    for pair in range(2):
        group = inputs[pair * 4 : pair * 4 + 4]
        for tile in range(2):
            slot = pair * 2 + tile
            ranks = [m[pl.ds(2 * CHANNELS * SLAB + tile * 8, 8), :] for m in group]
            parts = [[read_slab(m, (tile * CHANNELS + k) * SLAB) for k in range(CHANNELS)] for m in group]
            merged = merge_four(parts, ranks)
            for k in range(CHANNELS):
                write_slab(out, (slot * CHANNELS + k) * SLAB, merged[k])
            out[pl.ds(N * CHANNELS * SLAB + slot * 8, 8), :] = ranks[0]


def merge_x(messages):
    rows = N * CHANNELS * SLAB + N * 8
    vmem = pl.BlockSpec(memory_space=pltpu.VMEM)
    return pl.pallas_call(
        merge_x_kernel,
        in_specs=[vmem] * 8,
        out_specs=vmem,
        out_shape=jax.ShapeDtypeStruct((rows, LANES), jnp.float32),
        compiler_params=pltpu.CompilerParams(vmem_limit_bytes=VMEM),
        cost_estimate=pl.CostEstimate(flops=2**20, bytes_accessed=2**20, transcendentals=0),
        name="merge_x",
    )(*messages)


def merge_core_kernel(place, mine, other, out):
    core, z = place[2], place[3]
    for slot in range(N):
        where = N * CHANNELS * SLAB + slot * 8
        in_front = (mine[pl.ds(where, 8), :] < other[pl.ds(where, 8), :])[None]
        parts = [[read_slab(m, (slot * CHANNELS + k) * SLAB) for k in range(CHANNELS)] for m in (mine, other)]
        merged = merge_two(parts[0], parts[1], in_front)
        merged[3] = 1.0 - merged[3]
        tile = z ^ slot
        for k in range(CHANNELS):
            for block in range(BLOCKS):
                value = merged[k][block]
                value = jnp.where(core == 1, pltpu.roll(value, 4, 0), value)[:4]
                lanes = pl.ds(pl.multiple_of(tile * 512 + block * LANES, LANES), LANES)
                out[k, 0, :, lanes] = value


def merge_core(place, mine, other):
    vmem = pl.BlockSpec(memory_space=pltpu.VMEM)
    return pl.pallas_call(
        merge_core_kernel,
        in_specs=[pl.BlockSpec(memory_space=pltpu.SMEM), vmem, vmem],
        out_specs=vmem,
        out_shape=jax.ShapeDtypeStruct((CHANNELS, 1, 4, N * 512), jnp.float32),
        compiler_params=pltpu.CompilerParams(vmem_limit_bytes=VMEM),
        cost_estimate=pl.CostEstimate(flops=2**19, bytes_accessed=2**19, transcendentals=0),
        name="merge_core",
    )(place, mine, other)


def exchange(value, y=0, x=0, core=0, z=0):
    flip = ((y * N + x) * 2 + core) * N + z
    return lax.ppermute(value, ("depth", "tile"), [(i, i ^ flip) for i in range(N * N * 2 * N)])


def body(scalar_field, depth_rank, palette, extinction):
    depth = lax.axis_index("depth")
    place = jnp.stack([depth >> 3, (depth >> 1) & 3, depth & 1, lax.axis_index("tile")]).astype(jnp.int32)
    depth_total = scalar_field.shape[0] * lax.axis_size("depth")
    field = scalar_field.reshape(SAMPLES, 1, N, N, 2, 2, 8, 512)
    by_x = [None, None]
    for z_pair in (1, 0):
        received = {}
        for y_flips in ((2, 1), (3, 0)):
            sent = march(field, place, palette, extinction, depth_rank, y_flips, z_pair, depth_total)
            for j, flip in enumerate(y_flips):
                for tile in range(2):
                    z_flip = z_pair * 2 + tile
                    message = sent[j * 2 + tile]
                    received[tile, flip] = message if flip == z_flip == 0 else exchange(message, y=flip, z=z_flip)
        parts = merge_y(place, [received[tile, flip] for tile in range(2) for flip in range(N)])
        by_x[z_pair] = [parts[0]] + [exchange(parts[flip], x=flip) for flip in range(1, N)]
    mine = merge_x(by_x[0] + by_x[1])
    return merge_core(place, mine, exchange(mine, core=1))


def solution(mesh):
    in_specs = (P("depth", "tile", None, None), P("depth", "tile"), P(), P())
    out_specs = P(None, None, ("depth", "tile"), None)
    return jax.shard_map(body, mesh=mesh, in_specs=in_specs, out_specs=out_specs, check_vma=False)
```

```python
import functools
import math

import jax
import jax.numpy as jnp
from jax import lax
from jax.experimental import pallas as pl
from jax.experimental.pallas import tpu as pltpu
from jax.sharding import PartitionSpec as P

N = 4
SAMPLES = 16
LANES = 128
CHANNELS = 4
X_ROWS = 32
CORE_ROWS = 16
CHUNKS = ((0, 1), (2, 2), (1, 1))
GROUPS = ((0, 1), (2,))
VMEM = 40 * 2**20


def merge_two(a, b, a_in_front):
    one = jnp.float32(1.0)
    weight_a = jnp.where(a_in_front, one, b[3])
    weight_b = jnp.where(a_in_front, a[3], one)
    return [a[k] * weight_a + b[k] * weight_b for k in range(3)] + [a[3] * b[3]]


def merge_four(parts, ranks):
    even = merge_two(parts[0], parts[2], (ranks[0] < ranks[2])[None])
    odd = merge_two(parts[1], parts[3], (ranks[1] < ranks[3])[None])
    return merge_two(even, odd, (ranks[0] < ranks[1])[None])


def read(ref, start, rows):
    return ref[pl.ds(pl.multiple_of(start, 8), rows), :].reshape(rows // 8, 8, LANES)


def write(ref, start, value):
    ref[pl.ds(start, value.shape[0] * 8), :] = value.reshape(value.shape[0] * 8, LANES)


def vmem_specs(count):
    return [pl.BlockSpec(memory_space=pltpu.VMEM)] * count


def smem_specs(count):
    return [pl.BlockSpec(memory_space=pltpu.SMEM)] * count


def rows_of(*counts):
    return [jax.ShapeDtypeStruct((rows, LANES), jnp.float32) for rows in counts]


def cost(microseconds):
    return pl.CostEstimate(flops=int(microseconds * 1e9), bytes_accessed=1, transcendentals=0)


def march_kernel(place, slopes, extinction, rank, *refs, blocks, depth_total):
    fields, messages = refs[:N], refs[-N:]
    x = pl.program_id(0)
    scale = -1.0 / (depth_total * math.log(2.0))
    quadratic = extinction[0] * scale
    constant = extinction[1] * scale
    slope = [slopes[0, k] * 0.5 for k in range(3)]
    offset = [slopes[1, k] * 0.5 for k in range(3)]

    for field, message in zip(fields, messages):
        for block in range(blocks):
            shape = (X_ROWS, LANES)
            squares = jnp.zeros(shape, jnp.float32)
            through = jnp.ones(shape, jnp.float32)
            totals = [jnp.zeros(shape, jnp.float32) for _ in range(3)]
            for i in range(SAMPLES):
                s = field[i, :, block * LANES : (block + 1) * LANES]
                squares = squares + s * s
                after = jnp.exp2(squares * quadratic + constant * float(i + 1))
                weight = through - after
                through = after
                for k in range(3):
                    totals[k] = totals[k] + weight * jnp.tanh(s * slope[k] + offset[k])
            opacity = 1.0 - through
            channels = [0.5 * (opacity + totals[k]) for k in range(3)] + [through]
            for k in range(CHANNELS):
                row = ((k * N + x) * blocks + block) * X_ROWS
                message[pl.ds(pl.multiple_of(row, X_ROWS), X_ROWS), :] = channels[k]

    @pl.when(x == 0)
    def _():
        own = jnp.full((8, LANES), rank[0, 0].astype(jnp.float32))
        for message in messages:
            message[pl.ds(CHANNELS * N * blocks * X_ROWS, 8), :] = own


def march(field, place, palette, extinction, rank, first, blocks, depth_total, after=()):
    rows = CHANNELS * N * blocks * X_ROWS + 8

    def field_index(flip):
        return lambda x, where: (0, 0, (where[0] ^ flip) * N + x, first // blocks)

    return pl.pallas_call(
        functools.partial(march_kernel, blocks=blocks, depth_total=depth_total),
        grid_spec=pltpu.PrefetchScalarGridSpec(
            num_scalar_prefetch=1,
            grid=(N,),
            in_specs=smem_specs(3)
            + [pl.BlockSpec((SAMPLES, None, X_ROWS, blocks * LANES), field_index(flip)) for flip in range(N)]
            + [pl.BlockSpec(memory_space=pl.ANY)] * len(after),
            out_specs=[pl.BlockSpec((rows, LANES), lambda x, where: (0, 0))] * N,
        ),
        out_shape=rows_of(*[rows] * N),
        compiler_params=pltpu.CompilerParams(vmem_limit_bytes=VMEM),
        cost_estimate=cost(1.5 + 4.1 * blocks),
        name="march",
    )(place, palette.T, extinction, rank, *([field] * N), *after)


def merge_y_kernel(place, *refs, sizes):
    inputs, outputs = refs[:-N], refs[-N:]
    total = sum(sizes) * X_ROWS
    base = 0
    for c, blocks in enumerate(sizes):
        group = inputs[c * N : c * N + N]
        slab = blocks * X_ROWS
        ranks = [m[pl.ds(CHANNELS * N * slab, 8), :] for m in group]
        for flip in range(N):
            x = place[1] ^ flip
            parts = [[read(m, (k * N + x) * slab, slab) for k in range(CHANNELS)] for m in group]
            merged = merge_four(parts, ranks)
            for k in range(CHANNELS):
                write(outputs[flip], k * total + base, merged[k])
            outputs[flip][pl.ds(CHANNELS * total, 8), :] = ranks[0]
        base += slab


def merge_y(place, messages, sizes):
    return pl.pallas_call(
        functools.partial(merge_y_kernel, sizes=sizes),
        in_specs=smem_specs(1) + vmem_specs(len(messages)),
        out_specs=vmem_specs(N),
        out_shape=rows_of(*[CHANNELS * sum(sizes) * X_ROWS + 8] * N),
        compiler_params=pltpu.CompilerParams(vmem_limit_bytes=VMEM),
        cost_estimate=cost(0.3 * sum(sizes)),
        name="merge_y",
    )(place, *messages)


def merge_x_kernel(place, *refs):
    inputs, outputs = refs[:-2], refs[-2:]
    for g, chunks in enumerate(GROUPS):
        columns = [first + block for first, count in (CHUNKS[c] for c in chunks) for block in range(count)]
        group = inputs[g * N : g * N + N]
        blocks = len(columns)
        ranks = [m[pl.ds(CHANNELS * blocks * X_ROWS, 8), :] for m in group]
        for flip in range(2):
            core = place[2] ^ flip
            for block, column in enumerate(columns):
                parts = [
                    [read(m, (k * blocks + block) * X_ROWS + core * CORE_ROWS, CORE_ROWS) for k in range(CHANNELS)]
                    for m in group
                ]
                merged = merge_four(parts, ranks)
                for k in range(CHANNELS):
                    write(outputs[flip], (k * N + column) * CORE_ROWS, merged[k])
            outputs[flip][pl.ds(CHANNELS * N * CORE_ROWS, 8), :] = ranks[0]


def merge_x(place, messages):
    return pl.pallas_call(
        merge_x_kernel,
        in_specs=smem_specs(1) + vmem_specs(len(messages)),
        out_specs=vmem_specs(2),
        out_shape=rows_of(*[CHANNELS * N * CORE_ROWS + 8] * 2),
        compiler_params=pltpu.CompilerParams(vmem_limit_bytes=VMEM),
        cost_estimate=cost(0.5),
        name="merge_x",
    )(place, *messages)


def merge_core_kernel(place, mine, other, *targets):
    where = CHANNELS * N * CORE_ROWS
    in_front = (mine[pl.ds(where, 8), :] < other[pl.ds(where, 8), :])[None]
    for block in range(N):
        parts = [[read(m, (k * N + block) * CORE_ROWS, CORE_ROWS) for k in range(CHANNELS)] for m in (mine, other)]
        merged = merge_two(parts[0], parts[1], in_front)
        merged[3] = 1.0 - merged[3]
        for k in range(CHANNELS):
            for flip, target in enumerate(targets):
                z = place[3] ^ flip
                value = jnp.where(z >= 2, merged[k][1], merged[k][0])
                value = jnp.where((z & 1) == 1, pltpu.roll(value, 4, 0), value)
                target[pl.ds((k * N + block) * 4, 4), :] = value[:4]


def merge_core(place, mine, other):
    rows = CHANNELS * N * 4
    return pl.pallas_call(
        merge_core_kernel,
        in_specs=smem_specs(1) + vmem_specs(2),
        out_specs=vmem_specs(N),
        out_shape=rows_of(*[rows] * N),
        compiler_params=pltpu.CompilerParams(vmem_limit_bytes=VMEM),
        cost_estimate=cost(0.5),
        name="merge_core",
    )(place, mine, other)


def assemble_kernel(place, *refs):
    sources, out = refs[:N], refs[N]
    for flip, source in enumerate(sources):
        tile = place[3] ^ flip
        for k in range(CHANNELS):
            for block in range(N):
                lanes = pl.ds(pl.multiple_of((tile * N + block) * LANES, LANES), LANES)
                out[k, 0, :, lanes] = source[pl.ds((k * N + block) * 4, 4), :]


def assemble(place, pieces):
    return pl.pallas_call(
        assemble_kernel,
        in_specs=smem_specs(1) + vmem_specs(4),
        out_specs=pl.BlockSpec(memory_space=pltpu.VMEM),
        out_shape=jax.ShapeDtypeStruct((CHANNELS, 1, 4, N * N * LANES), jnp.float32),
        compiler_params=pltpu.CompilerParams(vmem_limit_bytes=VMEM),
        cost_estimate=cost(1.0),
        name="assemble",
    )(place, *pieces)


def exchange(value, y=0, x=0, core=0, z=0):
    flip = ((y * N + x) * 2 + core) * N + z
    return lax.ppermute(value, ("depth", "tile"), [(i, i ^ flip) for i in range(N * N * 2 * N)])


def all_flips(pieces, axis):
    moved = {flip: exchange(pieces[flip], **{axis: flip}) for flip in (2, 1, 3)}
    return [pieces[0], moved[1], moved[2], moved[3]]


def body(scalar_field, depth_rank, palette, extinction):
    depth = lax.axis_index("depth")
    place = jnp.stack([depth >> 3, (depth >> 1) & 3, depth & 1, lax.axis_index("tile")]).astype(jnp.int32)
    depth_total = scalar_field.shape[0] * lax.axis_size("depth")
    received, after = [], ()
    for c, (first, blocks) in enumerate(CHUNKS):
        sent = march(scalar_field, place, palette, extinction, depth_rank, first, blocks, depth_total, after)
        received.append(all_flips(sent, "y"))
        after = (sent[0],) if c == 0 else received[c - 1][1:]
    by_x = []
    for chunks in GROUPS:
        merged = merge_y(place, [m for c in chunks for m in received[c]], [CHUNKS[c][1] for c in chunks])
        by_x += all_flips(merged, "x")
    mine, send = merge_x(place, by_x)
    pieces = merge_core(place, mine, exchange(send, core=1))
    return assemble(place, all_flips(pieces, "z"))


def solution(mesh):
    in_specs = (P("depth", "tile", None, None), P("depth", "tile"), P(), P())
    out_specs = P(None, None, ("depth", "tile"), None)
    return jax.shard_map(body, mesh=mesh, in_specs=in_specs, out_specs=out_specs, check_vma=False)
```

```python
import functools
import math

import jax
import jax.numpy as jnp
from jax import lax
from jax.experimental import pallas as pl
from jax.experimental.pallas import tpu as pltpu
from jax.sharding import PartitionSpec as P

N = 4
SAMPLES = 16
LANES = 128
CHANNELS = 4
X_ROWS = 32
CORE_ROWS = 16
EARLY = 3
VMEM = 40 * 2**20


def merge_two(a, b, a_in_front):
    one = jnp.float32(1.0)
    weight_a = jnp.where(a_in_front, one, b[3])
    weight_b = jnp.where(a_in_front, a[3], one)
    return [a[k] * weight_a + b[k] * weight_b for k in range(3)] + [a[3] * b[3]]


def merge_four(parts, ranks):
    even = merge_two(parts[0], parts[2], (ranks[0] < ranks[2])[None])
    odd = merge_two(parts[1], parts[3], (ranks[1] < ranks[3])[None])
    return merge_two(even, odd, (ranks[0] < ranks[1])[None])


def read(ref, start, rows):
    return ref[pl.ds(pl.multiple_of(start, 8), rows), :].reshape(rows // 8, 8, LANES)


def write(ref, start, value):
    ref[pl.ds(start, value.shape[0] * 8), :] = value.reshape(value.shape[0] * 8, LANES)


def vmem_specs(count):
    return [pl.BlockSpec(memory_space=pltpu.VMEM)] * count


def smem_specs(count):
    return [pl.BlockSpec(memory_space=pltpu.SMEM)] * count


def rows_of(*counts):
    return [jax.ShapeDtypeStruct((rows, LANES), jnp.float32) for rows in counts]


def cost(microseconds):
    return pl.CostEstimate(flops=int(microseconds * 1e8), bytes_accessed=1, transcendentals=0)


def march_kernel(place, numbers, *refs, sizes, depth_total):
    fields, messages = refs[: len(sizes)], refs[-len(sizes) :]
    group = pl.program_id(0)
    scale = -1.0 / (depth_total * math.log(2.0))
    slope = [numbers[0, k] * 0.5 for k in range(3)]
    offset = [numbers[0, 3 + k] * 0.5 for k in range(3)]
    quadratic = numbers[0, 6] * scale
    constant = numbers[0, 7] * scale

    for field, message, blocks in zip(fields, messages, sizes):
        for block in range(blocks):
            shape = (X_ROWS, LANES)
            squares = jnp.zeros(shape, jnp.float32)
            through = jnp.ones(shape, jnp.float32)
            totals = [jnp.zeros(shape, jnp.float32) for _ in range(3)]
            for i in range(SAMPLES):
                s = field[i, :, block * LANES : (block + 1) * LANES]
                squares = squares + s * s
                after = jnp.exp2(squares * quadratic + constant * float(i + 1))
                weight = through - after
                through = after
                for k in range(3):
                    totals[k] = totals[k] + weight * jnp.tanh(s * slope[k] + offset[k])
            opacity = 1.0 - through
            channels = [0.5 * (opacity + totals[k]) for k in range(3)] + [through]
            for k in range(CHANNELS):
                row = ((k * N + group) * blocks + block) * X_ROWS
                message[pl.ds(pl.multiple_of(row, X_ROWS), X_ROWS), :] = channels[k]

    @pl.when(group == 0)
    def _():
        own = jnp.full((8, LANES), numbers[0, 8])
        for message, blocks in zip(messages, sizes):
            message[pl.ds(CHANNELS * N * blocks * X_ROWS, 8), :] = own


def march(field, place, numbers, parts, depth_total, after=()):
    def field_spec(axis, step, first, blocks):
        def index(group, where):
            y, x = (where[0] ^ step, group) if axis == "y" else (group, (where[1] + step) & 3)
            return 0, 0, y * N + x, first // blocks

        return pl.BlockSpec((SAMPLES, None, X_ROWS, blocks * LANES), index)

    sizes = [blocks for *_, blocks in parts]
    rows = [CHANNELS * N * blocks * X_ROWS + 8 for blocks in sizes]
    return pl.pallas_call(
        functools.partial(march_kernel, sizes=sizes, depth_total=depth_total),
        grid_spec=pltpu.PrefetchScalarGridSpec(
            num_scalar_prefetch=1,
            grid=(N,),
            in_specs=smem_specs(1)
            + [field_spec(*part) for part in parts]
            + [pl.BlockSpec(memory_space=pl.ANY)] * len(after),
            out_specs=[pl.BlockSpec((count, LANES), lambda group, where: (0, 0)) for count in rows],
        ),
        out_shape=rows_of(*rows),
        compiler_params=pltpu.CompilerParams(vmem_limit_bytes=VMEM),
        cost_estimate=cost(1.2 + 1.0 * sum(sizes)),
        name="march",
    )(place, numbers, *([field] * len(parts)), *after)


def turn_kernel(place, *refs):
    inputs, outputs = refs[:N], refs[N:]
    for brick, message in enumerate(inputs):
        for step in range(N):
            y = place[0] ^ step
            for k in range(CHANNELS):
                rows = message[pl.ds(pl.multiple_of((k * N + y) * X_ROWS, X_ROWS), X_ROWS), :]
                outputs[step][pl.ds((brick * CHANNELS + k) * X_ROWS, X_ROWS), :] = rows
            rank = message[pl.ds(CHANNELS * N * X_ROWS, 8), :]
            outputs[step][pl.ds(N * CHANNELS * X_ROWS + brick * 8, 8), :] = rank


def turn(place, messages):
    return pl.pallas_call(
        turn_kernel,
        in_specs=smem_specs(1) + vmem_specs(N),
        out_specs=vmem_specs(N),
        out_shape=rows_of(*[N * (CHANNELS * X_ROWS + 8)] * N),
        compiler_params=pltpu.CompilerParams(vmem_limit_bytes=VMEM),
        cost_estimate=cost(0.8),
        name="turn",
    )(place, *messages)


def merge_y_kernel(place, *refs):
    inputs, outputs = refs[:N], refs[-N:]
    slab = EARLY * X_ROWS
    ranks = [m[pl.ds(CHANNELS * N * slab, 8), :] for m in inputs]
    for step in range(N):
        x = (place[1] + step) & 3
        parts = [[read(m, (k * N + x) * slab, slab) for k in range(CHANNELS)] for m in inputs]
        merged = merge_four(parts, ranks)
        for k in range(CHANNELS):
            write(outputs[step], k * slab, merged[k])
        outputs[step][pl.ds(CHANNELS * slab, 8), :] = ranks[0]


def merge_y(place, messages, after=()):
    return pl.pallas_call(
        merge_y_kernel,
        in_specs=smem_specs(1) + vmem_specs(N) + [pl.BlockSpec(memory_space=pl.ANY)] * len(after),
        out_specs=vmem_specs(N),
        out_shape=rows_of(*[CHANNELS * EARLY * X_ROWS + 8] * N),
        compiler_params=pltpu.CompilerParams(vmem_limit_bytes=VMEM),
        cost_estimate=cost(0.9),
        name="merge_y",
    )(place, *messages, *after)


def merge_x_kernel(place, *refs):
    by_x, by_y, outputs = refs[:N], refs[N : 2 * N], refs[2 * N :]
    ranks = [m[pl.ds(CHANNELS * EARLY * X_ROWS, 8), :] for m in by_x]
    late_ranks = [[m[pl.ds(N * CHANNELS * X_ROWS + x * 8, 8), :] for m in by_y] for x in range(N)]
    for flip in range(2):
        core = place[2] ^ flip
        for block in range(EARLY):
            starts = [(k * EARLY + block) * X_ROWS + core * CORE_ROWS for k in range(CHANNELS)]
            merged = merge_four([[read(m, start, CORE_ROWS) for start in starts] for m in by_x], ranks)
            for k in range(CHANNELS):
                write(outputs[flip], (k * N + block) * CORE_ROWS, merged[k])
        bricks = []
        for x in range(N):
            starts = [(x * CHANNELS + k) * X_ROWS + core * CORE_ROWS for k in range(CHANNELS)]
            bricks.append(merge_four([[read(m, start, CORE_ROWS) for start in starts] for m in by_y], late_ranks[x]))
        merged = merge_four(bricks, [late_ranks[x][0] for x in range(N)])
        for k in range(CHANNELS):
            write(outputs[flip], (k * N + EARLY) * CORE_ROWS, merged[k])
        outputs[flip][pl.ds(CHANNELS * N * CORE_ROWS, 8), :] = ranks[0]


def merge_x(place, by_x, by_y):
    return pl.pallas_call(
        merge_x_kernel,
        in_specs=smem_specs(1) + vmem_specs(2 * N),
        out_specs=vmem_specs(2),
        out_shape=rows_of(*[CHANNELS * N * CORE_ROWS + 8] * 2),
        compiler_params=pltpu.CompilerParams(vmem_limit_bytes=VMEM),
        cost_estimate=cost(0.5),
        name="merge_x",
    )(place, *by_x, *by_y)


def merge_core_kernel(place, mine, other, *targets):
    where = CHANNELS * N * CORE_ROWS
    in_front = (mine[pl.ds(where, 8), :] < other[pl.ds(where, 8), :])[None]
    for block in range(N):
        parts = [[read(m, (k * N + block) * CORE_ROWS, CORE_ROWS) for k in range(CHANNELS)] for m in (mine, other)]
        merged = merge_two(parts[0], parts[1], in_front)
        merged[3] = 1.0 - merged[3]
        for k in range(CHANNELS):
            for step, target in enumerate(targets):
                z = (place[3] + step) & 3
                value = jnp.where(z >= 2, merged[k][1], merged[k][0])
                value = jnp.where((z & 1) == 1, pltpu.roll(value, 4, 0), value)
                target[pl.ds((k * N + block) * 4, 4), :] = value[:4]


def merge_core(place, mine, other):
    rows = CHANNELS * N * 4
    return pl.pallas_call(
        merge_core_kernel,
        in_specs=smem_specs(1) + vmem_specs(2),
        out_specs=vmem_specs(N),
        out_shape=rows_of(*[rows] * N),
        compiler_params=pltpu.CompilerParams(vmem_limit_bytes=VMEM),
        cost_estimate=cost(0.5),
        name="merge_core",
    )(place, mine, other)


def assemble_kernel(place, *refs):
    sources, out = refs[:N], refs[N]
    for step, source in enumerate(sources):
        tile = (place[3] - step) & 3
        for k in range(CHANNELS):
            for block in range(N):
                lanes = pl.ds(pl.multiple_of((tile * N + block) * LANES, LANES), LANES)
                out[k, 0, :, lanes] = source[pl.ds((k * N + block) * 4, 4), :]


def assemble(place, pieces):
    return pl.pallas_call(
        assemble_kernel,
        in_specs=smem_specs(1) + vmem_specs(4),
        out_specs=pl.BlockSpec(memory_space=pltpu.VMEM),
        out_shape=jax.ShapeDtypeStruct((CHANNELS, 1, 4, N * N * LANES), jnp.float32),
        compiler_params=pltpu.CompilerParams(vmem_limit_bytes=VMEM),
        cost_estimate=cost(1.0),
        name="assemble",
    )(place, *pieces)


def exchange(value, axis, step):
    def target(device):
        y, x, core, z = device // (2 * N * N), device // (2 * N) % N, device // N % 2, device % N
        if axis == "y":
            y ^= step
        elif axis == "x":
            x = (x + step) % N
        elif axis == "core":
            core ^= step
        else:
            z = (z + step) % N
        return ((y * N + x) * 2 + core) * N + z

    return lax.ppermute(value, ("depth", "tile"), [(i, target(i)) for i in range(2 * N * N * N)])


def all_steps(pieces, axis, order):
    moved = {step: exchange(pieces[step], axis, step) for step in order}
    return [pieces[0], moved[1], moved[2], moved[3]]


def body(scalar_field, depth_rank, palette, extinction):
    depth = lax.axis_index("depth")
    place = jnp.stack([depth >> 3, (depth >> 1) & 3, depth & 1, lax.axis_index("tile")]).astype(jnp.int32)
    slopes = palette.T
    rank = depth_rank.astype(jnp.float32)
    numbers = jnp.concatenate([slopes[0:1], slopes[1:2], extinction[None], rank], axis=1)
    depth_total = scalar_field.shape[0] * lax.axis_size("depth")
    (far,) = march(scalar_field, place, numbers, [("y", 2, 0, EARLY)], depth_total)
    parts = [("y", step, 0, EARLY) for step in (0, 1, 3)] + [("x", step, EARLY, 1) for step in range(N)]
    own, *near = march(scalar_field, place, numbers, parts, depth_total, [far])
    early = all_steps([own, near[0], far, near[1]], "y", (2, 1, 3))
    turned = turn(place, all_steps(near[2:], "x", (1, 2, 3)))
    by_x = all_steps(merge_y(place, early, turned[:1]), "x", (1, 2, 3))
    mine, send = merge_x(place, by_x, all_steps(turned, "y", (2, 1, 3)))
    pieces = merge_core(place, mine, exchange(send, "core", 1))
    return assemble(place, all_steps(pieces, "z", (2, 1, 3)))


def solution(mesh):
    in_specs = (P("depth", "tile", None, None), P("depth", "tile"), P(), P())
    out_specs = P(None, None, ("depth", "tile"), None)
    return jax.shard_map(body, mesh=mesh, in_specs=in_specs, out_specs=out_specs, check_vma=False)
```

```python
import functools
import math

import jax
import jax.numpy as jnp
from jax import lax
from jax.experimental import pallas as pl
from jax.experimental.pallas import tpu as pltpu
from jax.sharding import PartitionSpec as P

N = 4
SAMPLES = 16
LANES = 128
CHANNELS = 4
X_ROWS = 32
CORE_ROWS = 16
EARLY = 3
VMEM = 40 * 2**20


def merge_two(a, b, a_in_front):
    one = jnp.float32(1.0)
    weight_a = jnp.where(a_in_front, one, b[3])
    weight_b = jnp.where(a_in_front, a[3], one)
    return [a[k] * weight_a + b[k] * weight_b for k in range(3)] + [a[3] * b[3]]


def merge_four(parts, ranks):
    even = merge_two(parts[0], parts[2], (ranks[0] < ranks[2])[None])
    odd = merge_two(parts[1], parts[3], (ranks[1] < ranks[3])[None])
    return merge_two(even, odd, (ranks[0] < ranks[1])[None])


def read(ref, start, rows):
    return ref[pl.ds(pl.multiple_of(start, 8), rows), :].reshape(rows // 8, 8, LANES)


def write(ref, start, value):
    ref[pl.ds(start, value.shape[0] * 8), :] = value.reshape(value.shape[0] * 8, LANES)


def vmem_specs(count):
    return [pl.BlockSpec(memory_space=pltpu.VMEM)] * count


def smem_specs(count):
    return [pl.BlockSpec(memory_space=pltpu.SMEM)] * count


def rows_of(*counts):
    return [jax.ShapeDtypeStruct((rows, LANES), jnp.float32) for rows in counts]


def cost(microseconds):
    return pl.CostEstimate(flops=int(microseconds * 1e8), bytes_accessed=1, transcendentals=0)


def march_kernel(place, numbers, own_rank, *refs, sizes, depth_total):
    fields, messages = refs[: len(sizes)], refs[-len(sizes) :]
    group = pl.program_id(0)
    scale = -1.0 / (depth_total * math.log(2.0))
    slope = [numbers[0, 0, k] * 0.5 for k in range(3)]
    offset = [numbers[0, 1, k] * 0.5 for k in range(3)]
    quadratic = numbers[1, 0, 0] * scale
    constant = numbers[1, 1, 0] * scale

    for field, message, blocks in zip(fields, messages, sizes):
        for block in range(blocks):
            shape = (X_ROWS, LANES)
            squares = jnp.zeros(shape, jnp.float32)
            through = jnp.ones(shape, jnp.float32)
            totals = [jnp.zeros(shape, jnp.float32) for _ in range(3)]
            for i in range(SAMPLES):
                s = field[i, :, block * LANES : (block + 1) * LANES]
                squares = squares + s * s
                after = jnp.exp2(squares * quadratic + constant * float(i + 1))
                weight = through - after
                through = after
                for k in range(3):
                    totals[k] = totals[k] + weight * jnp.tanh(s * slope[k] + offset[k])
            opacity = 1.0 - through
            channels = [0.5 * (opacity + totals[k]) for k in range(3)] + [through]
            for k in range(CHANNELS):
                row = ((k * N + group) * blocks + block) * X_ROWS
                message[pl.ds(pl.multiple_of(row, X_ROWS), X_ROWS), :] = channels[k]

    @pl.when(group == 0)
    def _():
        own = jnp.full((8, LANES), own_rank[0, 0].astype(jnp.float32))
        for message, blocks in zip(messages, sizes):
            message[pl.ds(CHANNELS * N * blocks * X_ROWS, 8), :] = own


def march(field, place, parameters, parts, depth_total, after=()):
    def field_spec(axis, step, first, blocks):
        def index(group, where):
            y, x = (where[0] ^ step, group) if axis == "y" else (group, (where[1] + step) & 3)
            return 0, 0, y * N + x, first // blocks

        return pl.BlockSpec((SAMPLES, None, X_ROWS, blocks * LANES), index)

    sizes = [blocks for *_, blocks in parts]
    rows = [CHANNELS * N * blocks * X_ROWS + 8 for blocks in sizes]
    return pl.pallas_call(
        functools.partial(march_kernel, sizes=sizes, depth_total=depth_total),
        grid_spec=pltpu.PrefetchScalarGridSpec(
            num_scalar_prefetch=1,
            grid=(N,),
            in_specs=[
                pl.BlockSpec(v.shape, lambda group, where, v=v: (0,) * v.ndim, memory_space=pltpu.SMEM) for v in parameters
            ]
            + [field_spec(*part) for part in parts]
            + [pl.BlockSpec(memory_space=pl.ANY)] * len(after),
            out_specs=[pl.BlockSpec((count, LANES), lambda group, where: (0, 0)) for count in rows],
        ),
        out_shape=rows_of(*rows),
        compiler_params=pltpu.CompilerParams(vmem_limit_bytes=VMEM),
        cost_estimate=cost(1.2 + 1.0 * sum(sizes)),
        name="march",
    )(place, *parameters, *([field] * len(parts)), *after)


def turn_kernel(place, *refs):
    inputs, outputs = refs[:N], refs[N:]
    for brick, message in enumerate(inputs):
        for step in range(N):
            y = place[0] ^ step
            for k in range(CHANNELS):
                rows = message[pl.ds(pl.multiple_of((k * N + y) * X_ROWS, X_ROWS), X_ROWS), :]
                outputs[step][pl.ds((brick * CHANNELS + k) * X_ROWS, X_ROWS), :] = rows
            rank = message[pl.ds(CHANNELS * N * X_ROWS, 8), :]
            outputs[step][pl.ds(N * CHANNELS * X_ROWS + brick * 8, 8), :] = rank


def turn(place, messages):
    return pl.pallas_call(
        turn_kernel,
        in_specs=smem_specs(1) + vmem_specs(N),
        out_specs=vmem_specs(N),
        out_shape=rows_of(*[N * (CHANNELS * X_ROWS + 8)] * N),
        compiler_params=pltpu.CompilerParams(vmem_limit_bytes=VMEM),
        cost_estimate=cost(0.8),
        name="turn",
    )(place, *messages)


def merge_y_kernel(place, *refs):
    inputs, outputs = refs[:N], refs[-N:]
    slab = EARLY * X_ROWS
    ranks = [m[pl.ds(CHANNELS * N * slab, 8), :] for m in inputs]
    for step in range(N):
        x = (place[1] + step) & 3
        parts = [[read(m, (k * N + x) * slab, slab) for k in range(CHANNELS)] for m in inputs]
        merged = merge_four(parts, ranks)
        for k in range(CHANNELS):
            write(outputs[step], k * slab, merged[k])
        outputs[step][pl.ds(CHANNELS * slab, 8), :] = ranks[0]


def merge_y(place, messages, after=()):
    return pl.pallas_call(
        merge_y_kernel,
        in_specs=smem_specs(1) + vmem_specs(N) + [pl.BlockSpec(memory_space=pl.ANY)] * len(after),
        out_specs=vmem_specs(N),
        out_shape=rows_of(*[CHANNELS * EARLY * X_ROWS + 8] * N),
        compiler_params=pltpu.CompilerParams(vmem_limit_bytes=VMEM),
        cost_estimate=cost(0.9),
        name="merge_y",
    )(place, *messages, *after)


def merge_x_kernel(place, *refs):
    by_x, by_y, outputs = refs[:N], refs[N : 2 * N], refs[2 * N :]
    ranks = [m[pl.ds(CHANNELS * EARLY * X_ROWS, 8), :] for m in by_x]
    late_ranks = [[m[pl.ds(N * CHANNELS * X_ROWS + x * 8, 8), :] for m in by_y] for x in range(N)]
    for flip in range(2):
        core = place[2] ^ flip
        for block in range(EARLY):
            starts = [(k * EARLY + block) * X_ROWS + core * CORE_ROWS for k in range(CHANNELS)]
            merged = merge_four([[read(m, start, CORE_ROWS) for start in starts] for m in by_x], ranks)
            for k in range(CHANNELS):
                write(outputs[flip], (k * N + block) * CORE_ROWS, merged[k])
        bricks = []
        for x in range(N):
            starts = [(x * CHANNELS + k) * X_ROWS + core * CORE_ROWS for k in range(CHANNELS)]
            bricks.append(merge_four([[read(m, start, CORE_ROWS) for start in starts] for m in by_y], late_ranks[x]))
        merged = merge_four(bricks, [late_ranks[x][0] for x in range(N)])
        for k in range(CHANNELS):
            write(outputs[flip], (k * N + EARLY) * CORE_ROWS, merged[k])
        outputs[flip][pl.ds(CHANNELS * N * CORE_ROWS, 8), :] = ranks[0]


def merge_x(place, by_x, by_y):
    return pl.pallas_call(
        merge_x_kernel,
        in_specs=smem_specs(1) + vmem_specs(2 * N),
        out_specs=vmem_specs(2),
        out_shape=rows_of(*[CHANNELS * N * CORE_ROWS + 8] * 2),
        compiler_params=pltpu.CompilerParams(vmem_limit_bytes=VMEM),
        cost_estimate=cost(0.5),
        name="merge_x",
    )(place, *by_x, *by_y)


def merge_core_kernel(place, mine, other, *targets):
    where = CHANNELS * N * CORE_ROWS
    in_front = (mine[pl.ds(where, 8), :] < other[pl.ds(where, 8), :])[None]
    for block in range(N):
        parts = [[read(m, (k * N + block) * CORE_ROWS, CORE_ROWS) for k in range(CHANNELS)] for m in (mine, other)]
        merged = merge_two(parts[0], parts[1], in_front)
        merged[3] = 1.0 - merged[3]
        for k in range(CHANNELS):
            for step, target in enumerate(targets):
                z = (place[3] + step) & 3
                value = jnp.where(z >= 2, merged[k][1], merged[k][0])
                value = jnp.where((z & 1) == 1, pltpu.roll(value, 4, 0), value)
                target[pl.ds((k * N + block) * 4, 4), :] = value[:4]


def merge_core(place, mine, other):
    rows = CHANNELS * N * 4
    return pl.pallas_call(
        merge_core_kernel,
        in_specs=smem_specs(1) + vmem_specs(2),
        out_specs=vmem_specs(N),
        out_shape=rows_of(*[rows] * N),
        compiler_params=pltpu.CompilerParams(vmem_limit_bytes=VMEM),
        cost_estimate=cost(0.5),
        name="merge_core",
    )(place, mine, other)


def assemble_kernel(place, *refs):
    sources, out = refs[:N], refs[N]
    for step, source in enumerate(sources):
        tile = (place[3] - step) & 3
        for k in range(CHANNELS):
            for block in range(N):
                lanes = pl.ds(pl.multiple_of((tile * N + block) * LANES, LANES), LANES)
                out[k, 0, :, lanes] = source[pl.ds((k * N + block) * 4, 4), :]


def assemble(place, pieces):
    return pl.pallas_call(
        assemble_kernel,
        in_specs=smem_specs(1) + vmem_specs(4),
        out_specs=pl.BlockSpec(memory_space=pltpu.VMEM),
        out_shape=jax.ShapeDtypeStruct((CHANNELS, 1, 4, N * N * LANES), jnp.float32),
        compiler_params=pltpu.CompilerParams(vmem_limit_bytes=VMEM),
        cost_estimate=cost(1.0),
        name="assemble",
    )(place, *pieces)


def exchange(value, axis, step):
    def target(device):
        y, x, core, z = device // (2 * N * N), device // (2 * N) % N, device // N % 2, device % N
        if axis == "y":
            y ^= step
        elif axis == "x":
            x = (x + step) % N
        elif axis == "core":
            core ^= step
        else:
            z = (z + step) % N
        return ((y * N + x) * 2 + core) * N + z

    return lax.ppermute(value, ("depth", "tile"), [(i, target(i)) for i in range(2 * N * N * N)])


def all_steps(pieces, axis, order):
    moved = {step: exchange(pieces[step], axis, step) for step in order}
    return [pieces[0], moved[1], moved[2], moved[3]]


def body(scalar_field, depth_rank, palette, extinction):
    depth = lax.axis_index("depth")
    place = jnp.stack([depth >> 3, (depth >> 1) & 3, depth & 1, lax.axis_index("tile")]).astype(jnp.int32)
    which = lax.broadcasted_iota(jnp.int32, (2, 2, 3), 0)
    parameters = (jnp.where(which == 0, palette.T[None], extinction[None, :, None]), depth_rank)
    depth_total = scalar_field.shape[0] * lax.axis_size("depth")
    (far,) = march(scalar_field, place, parameters, [("y", 2, 0, EARLY)], depth_total)
    parts = [("y", step, 0, EARLY) for step in (0, 1, 3)] + [("x", step, EARLY, 1) for step in range(N)]
    own, *near = march(scalar_field, place, parameters, parts, depth_total, [far])
    early = all_steps([own, near[0], far, near[1]], "y", (2, 1, 3))
    turned = turn(place, all_steps(near[2:], "x", (1, 2, 3)))
    by_x = all_steps(merge_y(place, early, turned[:1]), "x", (1, 2, 3))
    mine, send = merge_x(place, by_x, all_steps(turned, "y", (2, 1, 3)))
    pieces = merge_core(place, mine, exchange(send, "core", 1))
    return assemble(place, all_steps(pieces, "z", (2, 1, 3)))


def solution(mesh):
    in_specs = (P("depth", "tile", None, None), P("depth", "tile"), P(), P())
    out_specs = P(None, None, ("depth", "tile"), None)
    return jax.shard_map(body, mesh=mesh, in_specs=in_specs, out_specs=out_specs, check_vma=False)
```

```python
import functools
import math

import jax
import jax.numpy as jnp
from jax import lax
from jax.experimental import pallas as pl
from jax.experimental.pallas import tpu as pltpu
from jax.sharding import PartitionSpec as P

N = 4
SAMPLES = 16
LANES = 128
CHANNELS = 4
X_ROWS = 32
CORE_ROWS = 16
EARLY = 3
VMEM = 40 * 2**20


def own_place():
    depth = lax.axis_index("depth")
    return depth >> 3, (depth >> 1) & 3, depth & 1, lax.axis_index("tile")


def merge_two(a, b, a_in_front):
    one = jnp.float32(1.0)
    weight_a = jnp.where(a_in_front, one, b[3])
    weight_b = jnp.where(a_in_front, a[3], one)
    return [a[k] * weight_a + b[k] * weight_b for k in range(3)] + [a[3] * b[3]]


def merge_four(parts, ranks):
    even = merge_two(parts[0], parts[2], (ranks[0] < ranks[2])[None])
    odd = merge_two(parts[1], parts[3], (ranks[1] < ranks[3])[None])
    return merge_two(even, odd, (ranks[0] < ranks[1])[None])


def read(ref, start, rows):
    return ref[pl.ds(pl.multiple_of(start, 8), rows), :].reshape(rows // 8, 8, LANES)


def write(ref, start, value):
    ref[pl.ds(start, value.shape[0] * 8), :] = value.reshape(value.shape[0] * 8, LANES)


def vmem_specs(count):
    return [pl.BlockSpec(memory_space=pltpu.VMEM)] * count


def smem_specs(count):
    return [pl.BlockSpec(memory_space=pltpu.SMEM)] * count


def rows_of(*counts):
    return [jax.ShapeDtypeStruct((rows, LANES), jnp.float32) for rows in counts]


def cost(microseconds):
    return pl.CostEstimate(flops=int(microseconds * 1e8), bytes_accessed=1, transcendentals=0)


def march_kernel(place, numbers, own_rank, *refs, sizes, depth_total):
    fields, messages = refs[: len(sizes)], refs[-len(sizes) :]
    group = pl.program_id(0)
    scale = -1.0 / (depth_total * math.log(2.0))
    slope = [numbers[0, 0, k] * 0.5 for k in range(3)]
    offset = [numbers[0, 1, k] * 0.5 for k in range(3)]
    quadratic = numbers[1, 0, 0] * scale
    constant = numbers[1, 1, 0] * scale

    for field, message, blocks in zip(fields, messages, sizes):
        for block in range(blocks):
            shape = (X_ROWS, LANES)
            squares = jnp.zeros(shape, jnp.float32)
            through = jnp.ones(shape, jnp.float32)
            totals = [jnp.zeros(shape, jnp.float32) for _ in range(3)]
            for i in range(SAMPLES):
                s = field[i, :, block * LANES : (block + 1) * LANES]
                squares = squares + s * s
                after = jnp.exp2(squares * quadratic + constant * float(i + 1))
                weight = through - after
                through = after
                for k in range(3):
                    totals[k] = totals[k] + weight * jnp.tanh(s * slope[k] + offset[k])
            opacity = 1.0 - through
            channels = [0.5 * (opacity + totals[k]) for k in range(3)] + [through]
            for k in range(CHANNELS):
                row = ((k * N + group) * blocks + block) * X_ROWS
                message[pl.ds(pl.multiple_of(row, X_ROWS), X_ROWS), :] = channels[k]

    @pl.when(group == 0)
    def _():
        own = jnp.full((8, LANES), own_rank[0, 0].astype(jnp.float32))
        for message, blocks in zip(messages, sizes):
            message[pl.ds(CHANNELS * N * blocks * X_ROWS, 8), :] = own


def march(field, place, parameters, parts, depth_total, after=()):
    def field_spec(axis, step, first, blocks):
        def index(group, where):
            y, x = (where[0] ^ step, group) if axis == "y" else (group, (where[1] + step) & 3)
            return 0, 0, y * N + x, first // blocks

        return pl.BlockSpec((SAMPLES, None, X_ROWS, blocks * LANES), index)

    sizes = [blocks for *_, blocks in parts]
    rows = [CHANNELS * N * blocks * X_ROWS + 8 for blocks in sizes]
    return pl.pallas_call(
        functools.partial(march_kernel, sizes=sizes, depth_total=depth_total),
        grid_spec=pltpu.PrefetchScalarGridSpec(
            num_scalar_prefetch=1,
            grid=(N,),
            in_specs=[
                pl.BlockSpec(v.shape, lambda group, where, v=v: (0,) * v.ndim, memory_space=pltpu.SMEM) for v in parameters
            ]
            + [field_spec(*part) for part in parts]
            + [pl.BlockSpec(memory_space=pl.ANY)] * len(after),
            out_specs=[pl.BlockSpec((count, LANES), lambda group, where: (0, 0)) for count in rows],
        ),
        out_shape=rows_of(*rows),
        compiler_params=pltpu.CompilerParams(vmem_limit_bytes=VMEM),
        cost_estimate=cost(1.2 + 1.0 * sum(sizes)),
        name="march",
    )(place, *parameters, *([field] * len(parts)), *after)


def turn_kernel(*refs):
    place = own_place()
    inputs, outputs = refs[:N], refs[N:]
    for brick, message in enumerate(inputs):
        for step in range(N):
            y = place[0] ^ step
            for k in range(CHANNELS):
                rows = message[pl.ds(pl.multiple_of((k * N + y) * X_ROWS, X_ROWS), X_ROWS), :]
                outputs[step][pl.ds((brick * CHANNELS + k) * X_ROWS, X_ROWS), :] = rows
            rank = message[pl.ds(CHANNELS * N * X_ROWS, 8), :]
            outputs[step][pl.ds(N * CHANNELS * X_ROWS + brick * 8, 8), :] = rank


def turn(messages):
    return pl.pallas_call(
        turn_kernel,
        in_specs=vmem_specs(N),
        out_specs=vmem_specs(N),
        out_shape=rows_of(*[N * (CHANNELS * X_ROWS + 8)] * N),
        compiler_params=pltpu.CompilerParams(vmem_limit_bytes=VMEM),
        cost_estimate=cost(0.8),
        name="turn",
    )(*messages)


def merge_pair_kernel(mine, other, out):
    slab = EARLY * X_ROWS
    rank = mine[pl.ds(CHANNELS * N * slab, 8), :]
    in_front = (rank < other[pl.ds(CHANNELS * N * slab, 8), :])[None]
    for x in range(N):
        starts = [(k * N + x) * slab for k in range(CHANNELS)]
        merged = merge_two(*[[read(m, start, slab) for start in starts] for m in (mine, other)], in_front)
        for start, value in zip(starts, merged):
            write(out, start, value)
    out[pl.ds(CHANNELS * N * slab, 8), :] = rank


def merge_pair(mine, other):
    return pl.pallas_call(
        merge_pair_kernel,
        in_specs=vmem_specs(2),
        out_specs=pl.BlockSpec(memory_space=pltpu.VMEM),
        out_shape=rows_of(CHANNELS * N * EARLY * X_ROWS + 8)[0],
        compiler_params=pltpu.CompilerParams(vmem_limit_bytes=VMEM),
        cost_estimate=cost(0.6),
        name="merge_pair",
    )(mine, other)


def merge_y_kernel(*refs):
    place = own_place()
    inputs, outputs = refs[:3], refs[-N:]
    slab = EARLY * X_ROWS
    ranks = [m[pl.ds(CHANNELS * N * slab, 8), :] for m in inputs]
    for step in range(N):
        x = (place[1] + step) & 3
        pair, *others = [[read(m, (k * N + x) * slab, slab) for k in range(CHANNELS)] for m in inputs]
        odd = merge_two(*others, (ranks[1] < ranks[2])[None])
        merged = merge_two(pair, odd, (ranks[0] < ranks[1])[None])
        for k in range(CHANNELS):
            write(outputs[step], k * slab, merged[k])
        outputs[step][pl.ds(CHANNELS * slab, 8), :] = ranks[0]


def merge_y(messages, after=()):
    return pl.pallas_call(
        merge_y_kernel,
        in_specs=vmem_specs(3) + [pl.BlockSpec(memory_space=pl.ANY)] * len(after),
        out_specs=vmem_specs(N),
        out_shape=rows_of(*[CHANNELS * EARLY * X_ROWS + 8] * N),
        compiler_params=pltpu.CompilerParams(vmem_limit_bytes=VMEM),
        cost_estimate=cost(0.9),
        name="merge_y",
    )(*messages, *after)


def merge_x_kernel(*refs):
    place = own_place()
    by_x, by_y, outputs = refs[:N], refs[N : 2 * N], refs[2 * N :]
    ranks = [m[pl.ds(CHANNELS * EARLY * X_ROWS, 8), :] for m in by_x]
    late_ranks = [[m[pl.ds(N * CHANNELS * X_ROWS + x * 8, 8), :] for m in by_y] for x in range(N)]
    for flip in range(2):
        core = place[2] ^ flip
        for block in range(EARLY):
            starts = [(k * EARLY + block) * X_ROWS + core * CORE_ROWS for k in range(CHANNELS)]
            merged = merge_four([[read(m, start, CORE_ROWS) for start in starts] for m in by_x], ranks)
            for k in range(CHANNELS):
                write(outputs[flip], (k * N + block) * CORE_ROWS, merged[k])
        bricks = []
        for x in range(N):
            starts = [(x * CHANNELS + k) * X_ROWS + core * CORE_ROWS for k in range(CHANNELS)]
            bricks.append(merge_four([[read(m, start, CORE_ROWS) for start in starts] for m in by_y], late_ranks[x]))
        merged = merge_four(bricks, [late_ranks[x][0] for x in range(N)])
        for k in range(CHANNELS):
            write(outputs[flip], (k * N + EARLY) * CORE_ROWS, merged[k])
        outputs[flip][pl.ds(CHANNELS * N * CORE_ROWS, 8), :] = ranks[0]


def merge_x(by_x, by_y):
    return pl.pallas_call(
        merge_x_kernel,
        in_specs=vmem_specs(2 * N),
        out_specs=vmem_specs(2),
        out_shape=rows_of(*[CHANNELS * N * CORE_ROWS + 8] * 2),
        compiler_params=pltpu.CompilerParams(vmem_limit_bytes=VMEM),
        cost_estimate=cost(0.5),
        name="merge_x",
    )(*by_x, *by_y)


def merge_core_kernel(mine, other, *targets):
    place = own_place()
    where = CHANNELS * N * CORE_ROWS
    in_front = (mine[pl.ds(where, 8), :] < other[pl.ds(where, 8), :])[None]
    for block in range(N):
        parts = [[read(m, (k * N + block) * CORE_ROWS, CORE_ROWS) for k in range(CHANNELS)] for m in (mine, other)]
        merged = merge_two(parts[0], parts[1], in_front)
        merged[3] = 1.0 - merged[3]
        for k in range(CHANNELS):
            for step, target in enumerate(targets):
                z = (place[3] + step) & 3
                value = jnp.where(z >= 2, merged[k][1], merged[k][0])
                value = jnp.where((z & 1) == 1, pltpu.roll(value, 4, 0), value)
                target[pl.ds((k * N + block) * 4, 4), :] = value[:4]


def merge_core(mine, other):
    rows = CHANNELS * N * 4
    return pl.pallas_call(
        merge_core_kernel,
        in_specs=vmem_specs(2),
        out_specs=vmem_specs(N),
        out_shape=rows_of(*[rows] * N),
        compiler_params=pltpu.CompilerParams(vmem_limit_bytes=VMEM),
        cost_estimate=cost(0.5),
        name="merge_core",
    )(mine, other)


def assemble_kernel(*refs):
    place = own_place()
    sources, out = refs[:N], refs[N]
    for step, source in enumerate(sources):
        tile = (place[3] - step) & 3
        for k in range(CHANNELS):
            for block in range(N):
                lanes = pl.ds(pl.multiple_of((tile * N + block) * LANES, LANES), LANES)
                out[k, 0, :, lanes] = source[pl.ds((k * N + block) * 4, 4), :]


def assemble(pieces):
    return pl.pallas_call(
        assemble_kernel,
        in_specs=vmem_specs(4),
        out_specs=pl.BlockSpec(memory_space=pltpu.VMEM),
        out_shape=jax.ShapeDtypeStruct((CHANNELS, 1, 4, N * N * LANES), jnp.float32),
        compiler_params=pltpu.CompilerParams(vmem_limit_bytes=VMEM),
        cost_estimate=cost(1.0),
        name="assemble",
    )(*pieces)


def exchange(value, axis, step):
    def target(device):
        y, x, core, z = device // (2 * N * N), device // (2 * N) % N, device // N % 2, device % N
        if axis == "y":
            y ^= step
        elif axis == "x":
            x = (x + step) % N
        elif axis == "core":
            core ^= step
        else:
            z = (z + step) % N
        return ((y * N + x) * 2 + core) * N + z

    return lax.ppermute(value, ("depth", "tile"), [(i, target(i)) for i in range(2 * N * N * N)])


def all_steps(pieces, axis, order):
    moved = {step: exchange(pieces[step], axis, step) for step in order}
    return [pieces[0], moved[1], moved[2], moved[3]]


def body(scalar_field, depth_rank, palette, extinction):
    place = jnp.stack(own_place()).astype(jnp.int32)
    which = lax.broadcasted_iota(jnp.int32, (2, 2, 3), 0)
    parameters = (jnp.where(which == 0, palette.T[None], extinction[None, :, None]), depth_rank)
    depth_total = scalar_field.shape[0] * lax.axis_size("depth")
    (far,) = march(scalar_field, place, parameters, [("y", 2, 0, EARLY)], depth_total)
    parts = [("y", step, 0, EARLY) for step in (0, 1, 3)] + [("x", step, EARLY, 1) for step in range(N)]
    own, *near = march(scalar_field, place, parameters, parts, depth_total, [far])
    early = all_steps([own, near[0], far, near[1]], "y", (2, 1, 3))
    turned = turn(all_steps(near[2:], "x", (1, 2, 3)))
    by_x = all_steps(merge_y([merge_pair(early[0], early[2]), early[1], early[3]], turned[:1]), "x", (1, 2, 3))
    mine, send = merge_x(by_x, all_steps(turned, "y", (2, 1, 3)))
    pieces = merge_core(mine, exchange(send, "core", 1))
    return assemble(all_steps(pieces, "z", (2, 1, 3)))


def solution(mesh):
    in_specs = (P("depth", "tile", None, None), P("depth", "tile"), P(), P())
    out_specs = P(None, None, ("depth", "tile"), None)
    return jax.shard_map(body, mesh=mesh, in_specs=in_specs, out_specs=out_specs, check_vma=False)
```
